32 devices in a mesh: dp: 4 (over z), ctx: 4 (over y, core), tensor: 2 (over x).
Axes of the slice: x: 2, y: 2, z: 4, core: 2. Of those that a mesh axis runs over, the one named last changes fastest.
Arguments:
- inputs: bfloat16 [2048, 8192], P(('dp', 'ctx')), may hold values from -6 to 6
- value_weight: bfloat16 [8192, 256], P(None, 'tensor'), may hold values from -0.0625 to 0.0625
- queries: bfloat16 [2048, 2048], P(('dp', 'ctx'), 'tensor'), may hold values from -8 to 8
- keys: bfloat16 [2048, 256], P(('dp', 'ctx'), 'tensor'), may hold values from -8 to 8
- out_grad: bfloat16 [2048, 2048], P(('dp', 'ctx'), 'tensor'), may hold values from -6 to 6
- doc_tiles: int32 [8, 3], P('dp'), may hold values from 1 to 12, 16 in all within a row
- route: int32 [4, 4, 4], P(None, 'ctx'), may hold values from 0 to 3, as said below
Outputs:
- query_grad: bfloat16 [2048, 2048], P(('dp', 'ctx'), 'tensor')
- key_grad: bfloat16 [2048, 256], P(('dp', 'ctx'), 'tensor')
- weight_grad: float32 [8192, 256], P(('dp', 'ctx'), 'tensor')
The draws below stay inside these ranges and needn't reach their ends.
Inputs may be any that keep to these rules, and one draw needn't show every extreme that they name: `doc_tiles`: each row sums to 16 and its largest entry is exactly 12. `route`: the 4 groups of one device go to 4 different data ranks, and at each context index every data rank takes exactly 4 groups.
All inputs are finite; a program needn't handle non-finite values.
Results may differ from the reference program's by a relative error of at most 0.012.
Values may be sent and summed in bfloat16 or wider, within the bound.
A program may use at most 64 MiB of HBM per device.

```python
import math
import jax
import jax.numpy as jnp
import numpy as np
from jax import lax

D = 8192
HEAD = 128
QPER = 8
TOK_DEV = 128
SEQS = 2
TILE = 16
NGRP = 4
DOCS = 3
KV_HEADS = 2
QH = 16
PACK = 256
PACK_TILES = 16
DOC_MOST = 12
BATCH_TOK = 2048
N_DP = 4
N_CTX = 4


def draw_keys(key, part):
    key = jax.random.fold_in(key, 1)
    result = jnp.clip(jax.random.normal(key, (BATCH_TOK, KV_HEADS * HEAD), jnp.float32), -6.0, 6.0)
    return result.astype(jnp.bfloat16)


def draw_queries(key, part):
    key = jax.random.fold_in(key, 3)
    result = jnp.clip(jax.random.normal(key, (BATCH_TOK, QH * HEAD), jnp.float32), -6.0, 6.0)
    return result.astype(jnp.bfloat16)


def draw_route(key, part):
    key = jax.random.fold_in(key, 5)

    def column_table(subkey):
        first_key, second_key = jax.random.split(subkey)
        shuffle = jax.random.permutation(first_key, N_DP).astype(jnp.int32)
        offsets = jax.random.permutation(second_key, N_DP - 1)[:NGRP - 1].astype(jnp.int32) + 1
        offsets = jnp.concatenate([jnp.zeros((1,), jnp.int32), offsets])
        sources = jnp.arange(N_DP, dtype=jnp.int32)
        return shuffle[(sources[:, None] + offsets[None, :]) % N_DP]
    tables = jax.vmap(column_table)(jax.random.split(key, N_CTX))
    return jnp.transpose(tables, (1, 0, 2)).astype(jnp.int32)


def strengthened(entries, rng, source, target, shards_of, factor):
    def block_of(dim):
        return (jnp.arange(entries.shape[dim]) // (entries.shape[dim] // shards_of)).reshape((-1,) + (1,) * (entries.ndim - 1 - dim))

    one_side = jax.random.permutation(rng, shards_of)[block_of(target)]
    other_side = (block_of(target) + shards_of // 2) % shards_of
    return jnp.where((block_of(source) == one_side) | (block_of(source) == other_side), factor * entries, entries)


def block_scale(own_key, extent, cuts, least, high):
    def one(dim, shards_of):
        steps = jax.random.uniform(jax.random.fold_in(jax.random.fold_in(own_key, 6), dim), (shards_of,), jnp.float32, least / len(cuts), high / len(cuts))
        return jnp.repeat(jnp.exp(steps), extent[dim] // shards_of).reshape((-1,) + (1,) * (len(extent) - dim - 1))

    loudness = one(*cuts[0])
    for cut in cuts[1:]:
        loudness = loudness * one(*cut)
    return loudness


def split_up(count, total, most, skew):
    portions = [(1 << 20) // math.isqrt(rank ** skew) + 1 for rank in range(2, count + 1)]
    spare, counts = total - most - (count - 1), [1] * (count - 1)
    while spare > 0:
        free = [i for i in range(count - 1) if counts[i] < most]
        pool, left = sum([portions[i] for i in free]), spare
        for i in free:
            addition = min(most - counts[i], max(1, left * portions[i] // pool), spare)
            counts[i] = counts[i] + addition
            spare = spare - addition
    return np.array([most] + counts)


def ragged(own_key, amount, total, reach, lean):
    if amount == 2:
        one = jax.random.randint(own_key, (), max(1, total - reach), min(reach, total - 1) + 1)
        return jnp.stack([one, total - one])
    sizes = jnp.asarray(split_up(amount, total, reach, lean), jnp.int32)
    couples = (amount - 1) // 2
    source_of, taker = sizes[1:1 + 2 * couples:2], sizes[2:2 + 2 * couples:2]
    slack = jnp.minimum(source_of - 1, reach - taker)
    shifted = jax.random.randint(jax.random.fold_in(own_key, 1), (couples,), 0, 1 << 20) % (slack + 1)
    sizes = sizes.at[1:1 + 2 * couples:2].set(source_of - shifted).at[2:2 + 2 * couples:2].set(taker + shifted)
    return sizes[jax.random.permutation(jax.random.fold_in(own_key, 2), amount)]


def bell_draw(rng, extent, scale, limit, cuts=(), held_as=jnp.bfloat16):
    array = jax.random.normal(rng, extent, jnp.float32) * scale
    if len(cuts) > 0:
        array = block_scale(rng, extent, cuts, -0.22, 0.18) * array
    return jnp.clip(array, min=-limit, max=limit).astype(held_as)


def bell_draw_with(stream_key, extent, scale, limit, shards, heavy, kind=jnp.bfloat16):
    values = scale * jax.random.normal(stream_key, extent, jnp.float32)
    if shards:
        values = values * block_scale(stream_key, extent, shards, -0.22, 0.18)
    return jnp.clip(strengthened(values, jax.random.fold_in(stream_key, 3), *heavy), -limit, limit).astype(kind)


def setup_inputs(seed: int = 0) -> dict:
    seeds = jax.random.split(jax.random.key(seed), 8)
    return {
        "inputs": bell_draw_with(seeds[0], (BATCH_TOK, D), 1.0, 6.0, ((0, 16),), (0, 1, 16, 2.0)),
        "value_weight": bell_draw(seeds[1], (D, KV_HEADS * HEAD), D ** -0.5, 0.0625, ((1, 2),)),
        "queries": draw_queries(jax.random.fold_in(seeds[7], 71), 0),
        "keys": draw_keys(jax.random.fold_in(seeds[7], 71), 0),
        "out_grad": bell_draw(seeds[4], (BATCH_TOK, QH * HEAD), 1.0, 6.0, ((0, 16), (1, 2))),
        "doc_tiles": jax.vmap(lambda own: ragged(own, DOCS, PACK_TILES, DOC_MOST, 2))(jax.random.split(seeds[5], (N_DP * SEQS))).reshape((N_DP * SEQS, DOCS)).astype(jnp.int32),
        "route": draw_route(jax.random.fold_in(seeds[7], 71), 0),
    }


def doc_numbers(positions, lengths):
    doc_ends = jnp.cumsum(lengths) * TILE
    return lax.optimization_barrier(jnp.sum((positions[:, None] >= doc_ends[None, :]).astype(jnp.int32), axis=1))

def group_tables(route):
    targets = jnp.arange(N_DP, dtype=jnp.int32)
    onehot = (route[:, :, :, None] == targets).astype(jnp.int32)
    send_counts = lax.optimization_barrier(jnp.sum(onehot, axis=2))
    before = jnp.cumsum(send_counts, axis=0) - send_counts
    arrival = lax.optimization_barrier(jnp.sum(onehot * before[:, :, None, :], axis=3))
    source = jnp.arange(N_DP, dtype=jnp.int32)[:, None, None]
    column = jnp.arange(N_CTX, dtype=jnp.int32)[None, :, None]
    member = jnp.arange(NGRP, dtype=jnp.int32)[None, None, :]
    moved_index = ((route * N_CTX + column) * NGRP + arrival).reshape(-1)
    home_index = ((source * N_CTX + column) * NGRP + member + 0 * route).reshape(-1)
    group_total = N_DP * N_CTX * NGRP
    forward = jnp.zeros((group_total,), jnp.int32).at[moved_index].set(home_index)
    backward = jnp.zeros((group_total,), jnp.int32).at[home_index].set(moved_index)
    return (forward, backward)

def regroup(rows_array, order_index):
    group_rows = TOK_DEV // NGRP
    pieces = rows_array.reshape(N_DP * N_CTX * NGRP, group_rows, rows_array.shape[1])
    return jnp.take(pieces, order_index, axis=0).reshape(rows_array.shape)

def to_packs(rows_array):
    seg_rows = TOK_DEV // SEQS
    shaped = rows_array.reshape(N_DP, N_CTX, SEQS, seg_rows, rows_array.shape[1])
    return jnp.transpose(shaped, (0, 2, 1, 3, 4)).reshape(N_DP * SEQS, PACK, rows_array.shape[1])

def from_packs(pack_array):
    seg_rows = TOK_DEV // SEQS
    shaped = pack_array.reshape(N_DP, SEQS, N_CTX, seg_rows, pack_array.shape[2])
    return jnp.transpose(shaped, (0, 2, 1, 3, 4)).reshape(BATCH_TOK, pack_array.shape[2])

def head_group(operands):
    query_block, key_block, value_block, grad_block, lengths = operands
    positions = jnp.arange(PACK, dtype=jnp.int32)
    documents = doc_numbers(positions, lengths)
    allowed = (documents[:, None] == documents[None, :]) & (positions[None, :] <= positions[:, None])
    score_scale = 1.0 / math.sqrt(HEAD)
    query_float = query_block.astype(jnp.float32)
    key_float = key_block.astype(jnp.float32)
    value_float = value_block.astype(jnp.float32)
    grad_float = grad_block.astype(jnp.float32)
    scores = jnp.einsum('qhd,kd->hqk', query_float, key_float) * score_scale
    scores = jnp.where(allowed[None], scores, -jnp.inf)
    row_peak = lax.optimization_barrier(jnp.max(scores, axis=2, keepdims=True))
    weights = jnp.exp(scores - row_peak)
    attention = weights / lax.optimization_barrier(jnp.sum(weights, axis=2, keepdims=True))
    attention_low = attention.astype(jnp.bfloat16)
    low_float = attention_low.astype(jnp.float32)
    attended = jnp.einsum('hqk,kd->qhd', low_float, value_float).astype(jnp.bfloat16)
    row_inner = lax.optimization_barrier(jnp.sum(grad_float * attended.astype(jnp.float32), axis=2))
    grad_probs = jnp.einsum('qhd,kd->hqk', grad_float, value_float)
    grad_scores = (attention * (grad_probs - jnp.transpose(row_inner)[:, :, None]) * score_scale).astype(jnp.bfloat16)
    score_float = grad_scores.astype(jnp.float32)
    query_grad = jnp.einsum('hqk,kd->qhd', score_float, key_float).astype(jnp.bfloat16)
    key_grad = jnp.einsum('hqk,qhd->kd', score_float, query_float).astype(jnp.bfloat16)
    value_grad = jnp.einsum('hqk,qhd->kd', low_float, grad_float).astype(jnp.bfloat16)
    return (query_grad, key_grad, value_grad)

def reference(inputs, value_weight, queries, keys, out_grad, doc_tiles, route):
    values = jnp.dot(inputs, value_weight, preferred_element_type=jnp.float32).astype(jnp.bfloat16)
    forward, backward = group_tables(route)
    moved_queries = regroup(queries, forward)
    moved_keys = regroup(keys, forward)
    moved_values = regroup(values, forward)
    group_count = keys.shape[1] // HEAD
    pack_count = N_DP * SEQS

    def split_heads(rows_array, per_group):
        shaped = to_packs(rows_array).reshape(pack_count, PACK, group_count, per_group, HEAD)
        return jnp.transpose(shaped, (0, 2, 1, 3, 4)).reshape(pack_count * group_count, PACK, per_group, HEAD)

    def join_heads(stacked, per_group):
        shaped = stacked.reshape(pack_count, group_count, PACK, per_group, HEAD)
        joined = jnp.transpose(shaped, (0, 2, 1, 3, 4)).reshape(pack_count, PACK, group_count * per_group * HEAD)
        return from_packs(joined)
    query_sets = split_heads(moved_queries, QPER)
    key_sets = split_heads(moved_keys, 1)[:, :, 0]
    value_sets = split_heads(moved_values, 1)[:, :, 0]
    grad_sets = split_heads(out_grad, QPER)
    length_sets = jnp.repeat(doc_tiles, group_count, axis=0)
    query_grads, key_grads, value_grads = lax.map(head_group, (query_sets, key_sets, value_sets, grad_sets, length_sets))
    query_grad = regroup(join_heads(query_grads, QPER), backward)
    key_grad = regroup(join_heads(key_grads[:, :, None], 1), backward)
    value_grad = regroup(join_heads(value_grads[:, :, None], 1), backward)
    weight_grad = jnp.dot(inputs.T, value_grad, preferred_element_type=jnp.float32)
    return (query_grad, key_grad, weight_grad)
```

```python
import functools
import math

import jax
import jax.numpy as jnp
from jax import lax
from jax.experimental import pallas as pl
from jax.experimental.pallas import tpu as pltpu
from jax.sharding import PartitionSpec as P

TILE = 16
CHUNKS = 4
BF16 = jnp.bfloat16
F32 = jnp.float32
KV, Q, DQ, DKV, WG = range(5)
GATHER, REDUCE, VGRAD = range(3)


def contract_rows(left, right):
    return lax.dot_general(left, right, (((0,), (0,)), ((), ())), preferred_element_type=F32)


def contract_lanes(left, right):
    return lax.dot_general(left, right, (((1,), (1,)), ((), ())), preferred_element_type=F32)


def pick(flags, pieces):
    total = flags[0] * pieces[0].astype(F32)
    for flag, piece in zip(flags[1:], pieces[1:]):
        total = total + flag * piece.astype(F32)
    return total.astype(BF16)


def kernel(
    data, ctx, x_ref, cols_ref, w_ref, q_ref, k_ref, g_ref, doc_ref, route_ref,
    qg_ref, kg_ref, wg_ref,
    x_buf, w_buf, kv_send, kv_recv, q_send, q_recv, kv_all, x_recv,
    red_send, red_recv, dq_send, dq_recv, dkv_send, dkv_recv, vg_all, wg_send, wg_recv,
    load_sem, own_sem, dp_send_sem, dp_recv_sem, ctx_send_sem, ctx_recv_sem, x_send_sem, x_recv_sem,
):
    rank, col = lax.axis_index("dp"), lax.axis_index("ctx")
    rows, head = k_ref.shape
    width = q_ref.shape[1]
    heads = width // head
    groups = route_ref.shape[1]
    size = rows // groups
    packs, docs = doc_ref.shape
    seg = rows // packs
    block = wg_ref.shape[0]
    depth = x_ref.shape[1]
    step = depth // CHUNKS
    direct = groups == data
    aligned = block % 128 == 0
    ranks = [lax.rem(rank + i, data) for i in range(data)]
    cols = [lax.rem(col + i, ctx) for i in range(ctx)]

    def to_rank(phase, i, src, dst):
        return pltpu.make_async_remote_copy(
            src_ref=src, dst_ref=dst, send_sem=dp_send_sem.at[phase, i],
            recv_sem=dp_recv_sem.at[phase, i], device_id={"dp": ranks[i]},
            device_id_type=pl.DeviceIdType.MESH)

    def to_col(phase, i, src, dst):
        return pltpu.make_async_remote_copy(
            src_ref=src, dst_ref=dst, send_sem=ctx_send_sem.at[phase, i],
            recv_sem=ctx_recv_sem.at[phase, i], device_id={"ctx": cols[i]},
            device_id_type=pl.DeviceIdType.MESH)

    barrier = pltpu.get_barrier_semaphore()
    for i in range(1, data):
        pl.semaphore_signal(barrier, inc=1, device_id={"dp": ranks[i]}, device_id_type=pl.DeviceIdType.MESH)
    for i in range(1, ctx):
        pl.semaphore_signal(barrier, inc=1, device_id={"ctx": cols[i]}, device_id_type=pl.DeviceIdType.MESH)

    loads = []
    for n in range(CHUNKS):
        span = pl.ds(n * step, step)
        loads.append((
            pltpu.make_async_copy(x_ref.at[:, span], x_buf.at[:, span], load_sem.at[0, n]),
            pltpu.make_async_copy(w_ref.at[span, :], w_buf.at[span, :], load_sem.at[1, n])))
        for load in loads[-1]:
            load.start()

    going = [[(route_ref[rank, j] == ranks[i]).astype(F32) for j in range(groups)] for i in range(data)]
    if not direct:
        placed, before = [], 0
        for s in range(data):
            count = 0
            for j in range(groups):
                count = count + (route_ref[s, j] == rank).astype(jnp.int32)
            placed.append([((before == k) & (count > 0)).astype(F32) for k in range(groups)])
            before = before + count

    def parts(array):
        return [array[j * size:(j + 1) * size] for j in range(groups)]

    q_parts, k_parts = parts(q_ref[...]), parts(k_ref[...])
    for i in range(data):
        piece = pick(going[i], q_parts)
        if i == 0:
            q_recv[rank] = piece
        else:
            q_send[i] = piece
    values = jnp.zeros((rows, head), F32)
    for n in range(CHUNKS):
        for load in loads[n]:
            load.wait()
        values = values + jnp.dot(
            x_buf[:, n * step:(n + 1) * step], w_buf[n * step:(n + 1) * step, :],
            preferred_element_type=F32)
    v_parts = parts(values.astype(BF16))
    for i in range(data):
        piece = jnp.concatenate([pick(going[i], k_parts), pick(going[i], v_parts)], axis=1)
        if i == 0:
            kv_recv[rank] = piece
        else:
            kv_send[i] = piece

    pl.semaphore_wait(barrier, data - 1 + ctx - 1)

    kv_out = [to_rank(KV, i, kv_send.at[i], kv_recv.at[rank]) for i in range(1, data)]
    q_out = [to_rank(Q, i, q_send.at[i], q_recv.at[rank]) for i in range(1, data)]
    for copy in kv_out + q_out:
        copy.start()
    x_out, x_own = [], []
    for d in range(data if aligned else 1):
        for i in range(ctx):
            if aligned:
                start = pl.multiple_of((d * ctx + cols[i]) * block, block)
                source = x_buf.at[:, pl.ds(start, block)]
            else:
                source = cols_ref.at[cols[i]]
            if i == 0:
                x_own.append(pltpu.make_async_copy(source, x_recv.at[d, col], own_sem.at[d]))
            else:
                x_out.append(pltpu.make_async_remote_copy(
                    src_ref=source, dst_ref=x_recv.at[d, col],
                    send_sem=x_send_sem.at[d, i], recv_sem=x_recv_sem.at[d, i],
                    device_id={"ctx": cols[i]}, device_id_type=pl.DeviceIdType.MESH))
    for copy in x_own:
        copy.start()

    def arrange(buffer):
        if direct:
            return buffer[...].reshape(rows, buffer.shape[2])
        pieces = [buffer[s] for s in range(data)]
        return jnp.concatenate(
            [pick([placed[s][k] for s in range(data)], pieces) for k in range(groups)], axis=0)

    for copy in kv_out:
        copy.wait_recv()
    kv_all[col] = arrange(kv_recv)
    gather = [to_col(GATHER, i, kv_all.at[col], kv_all.at[col]) for i in range(1, ctx)]
    for copy in gather:
        copy.start()
    for copy in x_out:
        copy.start()
    for copy in q_out:
        copy.wait_recv()
    queries = arrange(q_recv)
    for copy in gather:
        copy.wait_recv()

    scale = 1.0 / math.sqrt(head)
    pack_len = ctx * seg

    def stack(array, p):
        return jnp.concatenate(
            [array[p * seg:(p + 1) * seg, h * head:(h + 1) * head] for h in range(heads)], axis=0)

    scores_grad, query_stacks, key_stacks = [], [], []
    for p in range(packs):
        pair = kv_all[:, p * seg:(p + 1) * seg, :].reshape(pack_len, 2 * head)
        keys, vals = pair[:, :head], pair[:, head:]
        query_pos = col * seg + lax.broadcasted_iota(jnp.int32, (seg, pack_len), 0)
        key_pos = lax.broadcasted_iota(jnp.int32, (seg, pack_len), 1)
        query_doc, key_doc, end = jnp.zeros_like(query_pos), jnp.zeros_like(key_pos), 0
        for n in range(docs):
            end = end + doc_ref[p, n] * TILE
            query_doc = query_doc + jnp.where(query_pos >= end, 1, 0)
            key_doc = key_doc + jnp.where(key_pos >= end, 1, 0)
        bias = jnp.where((query_doc == key_doc) & (key_pos <= query_pos), 0.0, -1e30)
        query_stack, grad_stack = stack(queries, p), stack(g_ref, p)
        scores = contract_lanes(query_stack, keys) * scale
        scores = (scores.reshape(heads, seg, pack_len) + bias[None]).reshape(heads * seg, pack_len)
        weights = jnp.exp(scores - jnp.max(scores, axis=1, keepdims=True))
        probs = weights * (1.0 / jnp.sum(weights, axis=1, keepdims=True))
        grad_probs = contract_lanes(grad_stack, vals)
        inner = jnp.sum(probs * grad_probs, axis=1, keepdims=True)
        ds = (probs * (grad_probs - inner) * scale).astype(BF16)
        dk = contract_rows(ds, query_stack).astype(BF16)
        dv = contract_rows(probs.astype(BF16), grad_stack).astype(BF16)
        red_send[:, p * seg:(p + 1) * seg, :head] = dk.reshape(ctx, seg, head)
        red_send[:, p * seg:(p + 1) * seg, head:] = dv.reshape(ctx, seg, head)
        scores_grad.append(ds)
        key_stacks.append(keys)
    reduce = [to_col(REDUCE, i, red_send.at[cols[i]], red_recv.at[i]) for i in range(1, ctx)]
    for copy in reduce:
        copy.start()

    halves = []
    for p in range(packs):
        dq = jnp.dot(scores_grad[p], key_stacks[p], preferred_element_type=F32).astype(BF16)
        halves.append(jnp.concatenate([dq[h * seg:(h + 1) * seg] for h in range(heads)], axis=1))
    dq_rows = jnp.concatenate(halves, axis=0)

    def hand_back(array, send, recv, phase):
        if direct:
            send[...] = array.reshape(send.shape)
            recv[rank] = send[rank]
            copies = [to_rank(phase, i, send.at[ranks[i]], recv.at[rank]) for i in range(1, data)]
        else:
            pieces = parts(array)
            for s in range(data):
                send[s] = pick(placed[s], pieces)
            recv[rank] = send[rank]
            copies = [to_rank(phase, i, send.at[ranks[i]], recv.at[rank]) for i in range(1, data)]
        for copy in copies:
            copy.start()
        return copies

    def restore(recv):
        pieces = [recv[ranks[i]] for i in range(data)]
        return jnp.concatenate(
            [pick([going[i][j] for i in range(data)], pieces) for j in range(groups)], axis=0)

    dq_out = hand_back(dq_rows, dq_send, dq_recv, DQ)

    total = red_send[col].astype(F32)
    for copy in reduce:
        copy.wait_recv()
    for i in range(1, ctx):
        total = total + red_recv[i].astype(F32)
    dkv_out = hand_back(total.astype(BF16), dkv_send, dkv_recv, DKV)
    for copy in dkv_out:
        copy.wait_recv()
    dkv = restore(dkv_recv)
    vg_all[col] = dkv[:, head:]
    vgrad = [to_col(VGRAD, i, vg_all.at[col], vg_all.at[col]) for i in range(1, ctx)]
    for copy in vgrad:
        copy.start()
    kg_ref[...] = dkv[:, :head]
    for copy in x_out:
        copy.wait_recv()
    for copy in x_own:
        copy.wait()
    for copy in vgrad:
        copy.wait_recv()
    value_grad = vg_all[...].reshape(ctx * rows, head)
    wg_out = []
    if not aligned:
        terms = contract_rows(x_recv[0].reshape(ctx * rows, data * block), value_grad)
        wg_send[...] = terms.astype(BF16).reshape(wg_send.shape)
    for i in range(1, data):
        if aligned:
            term = contract_rows(value_grad, x_recv[ranks[i]].reshape(ctx * rows, block))
            wg_send[ranks[i]] = term.astype(BF16)
        copy = to_rank(WG, i, wg_send.at[ranks[i]], wg_recv.at[i])
        copy.start()
        wg_out.append(copy)
    if aligned:
        weight_grad = contract_rows(value_grad, x_recv[rank].reshape(ctx * rows, block))
    else:
        weight_grad = wg_send[rank].astype(F32)
    for copy in dq_out:
        copy.wait_recv()
    qg_ref[...] = restore(dq_recv)
    for copy in wg_out:
        copy.wait_recv()
    for i in range(1, data):
        weight_grad = weight_grad + wg_recv[i].astype(F32)
    wg_ref[...] = weight_grad.T if aligned else weight_grad
    for copy in kv_out + q_out + x_out + gather + reduce + dq_out + dkv_out + vgrad + wg_out:
        copy.wait_send()


def local(inputs, value_weight, queries, keys, out_grad, doc_tiles, route):
    data, ctx = lax.axis_size("dp"), lax.axis_size("ctx")
    rows, depth = inputs.shape
    head, width = keys.shape[1], queries.shape[1]
    groups = route.shape[2]
    size = rows // groups
    block = depth // (data * ctx)
    columns, blocks, term = inputs, (data, ctx, rows, block), (data, head, block)
    if block % 128:
        columns = jnp.transpose(inputs.reshape(rows, data, ctx, block), (2, 0, 1, 3))
        columns = columns.reshape(ctx, rows, data * block)
        blocks, term = (1, ctx, rows, data * block), (data, block, head)
    vmem = pl.BlockSpec(memory_space=pltpu.VMEM)
    smem = pl.BlockSpec(memory_space=pltpu.SMEM)
    anywhere = pl.BlockSpec(memory_space=pl.ANY)
    dma = pltpu.SemaphoreType.DMA
    return pl.pallas_call(
        functools.partial(kernel, data, ctx),
        out_shape=(
            jax.ShapeDtypeStruct((rows, width), BF16),
            jax.ShapeDtypeStruct((rows, head), BF16),
            jax.ShapeDtypeStruct((block, head), F32)),
        in_specs=[anywhere, anywhere, anywhere, vmem, vmem, vmem, smem, smem],
        out_specs=(vmem, vmem, vmem),
        scratch_shapes=[
            pltpu.VMEM((rows, depth), BF16),
            pltpu.VMEM((depth, head), BF16),
            pltpu.VMEM((data, size, 2 * head), BF16),
            pltpu.VMEM((data, size, 2 * head), BF16),
            pltpu.VMEM((data, size, width), BF16),
            pltpu.VMEM((data, size, width), BF16),
            pltpu.VMEM((ctx, rows, 2 * head), BF16),
            pltpu.VMEM(blocks, BF16),
            pltpu.VMEM((ctx, rows, 2 * head), BF16),
            pltpu.VMEM((ctx, rows, 2 * head), BF16),
            pltpu.VMEM((data, size, width), BF16),
            pltpu.VMEM((data, size, width), BF16),
            pltpu.VMEM((data, size, 2 * head), BF16),
            pltpu.VMEM((data, size, 2 * head), BF16),
            pltpu.VMEM((ctx, rows, head), BF16),
            pltpu.VMEM(term, BF16),
            pltpu.VMEM(term, BF16),
            dma((2, CHUNKS)), dma((data,)),
            dma((5, data)), dma((5, data)), dma((3, ctx)), dma((3, ctx)),
            dma((data, ctx)), dma((data, ctx)),
        ],
        compiler_params=pltpu.CompilerParams(
            collective_id=0, has_side_effects=True, vmem_limit_bytes=48 * 1024 * 1024),
    )(inputs, columns, value_weight, queries, keys, out_grad, doc_tiles, route[:, 0, :])


def solution(mesh):
    in_specs = (
        P(("dp", "ctx"), None),
        P(None, "tensor"),
        P(("dp", "ctx"), "tensor"),
        P(("dp", "ctx"), "tensor"),
        P(("dp", "ctx"), "tensor"),
        P("dp", None),
        P(None, "ctx", None),
    )
    out_specs = (P(("dp", "ctx"), "tensor"), P(("dp", "ctx"), "tensor"), P(("dp", "ctx"), "tensor"))
    return jax.shard_map(local, mesh=mesh, in_specs=in_specs, out_specs=out_specs, check_vma=False)
```

```python
import functools
import math

import jax
import jax.numpy as jnp
from jax import lax
from jax.experimental import pallas as pl
from jax.experimental.pallas import tpu as pltpu
from jax.sharding import PartitionSpec as P

TILE = 16
CHUNKS = 4
BF16 = jnp.bfloat16
F32 = jnp.float32
KV, Q, DQ, DKV, WG = range(5)
GATHER, REDUCE, VGRAD = range(3)


def contract_rows(left, right):
    return lax.dot_general(left, right, (((0,), (0,)), ((), ())), preferred_element_type=F32)


def contract_lanes(left, right):
    return lax.dot_general(left, right, (((1,), (1,)), ((), ())), preferred_element_type=F32)


def pick(flags, pieces):
    total = flags[0] * pieces[0].astype(F32)
    for flag, piece in zip(flags[1:], pieces[1:]):
        total = total + flag * piece.astype(F32)
    return total.astype(BF16)


def kernel(
    data, ctx, x_ref, cols_ref, w_ref, q_hbm, k_hbm, g_hbm, doc_hbm, route_hbm,
    qg_ref, kg_ref, wg_ref,
    x_buf, w_buf, q_ref, k_ref, g_ref, doc_ref, route_ref, kv_send, kv_recv, q_send, q_recv, kv_all, x_recv,
    red_send, red_recv, dq_send, dq_recv, dkv_send, dkv_recv, vg_all, wg_send, wg_recv,
    load_sem, small_sem, own_sem, dp_send_sem, dp_recv_sem, ctx_send_sem, ctx_recv_sem, x_send_sem, x_recv_sem,
):
    rank, col = lax.axis_index("dp"), lax.axis_index("ctx")
    rows, head = k_ref.shape
    width = q_ref.shape[1]
    heads = width // head
    groups = route_ref.shape[2]
    size = rows // groups
    packs, docs = doc_ref.shape
    seg = rows // packs
    block = wg_ref.shape[0]
    depth = x_ref.shape[1]
    step = depth // CHUNKS
    direct = groups == data
    aligned = block % 128 == 0
    ranks = [lax.rem(rank + i, data) for i in range(data)]
    cols = [lax.rem(col + i, ctx) for i in range(ctx)]

    def to_rank(phase, i, src, dst):
        return pltpu.make_async_remote_copy(
            src_ref=src, dst_ref=dst, send_sem=dp_send_sem.at[phase, i],
            recv_sem=dp_recv_sem.at[phase, i], device_id={"dp": ranks[i]},
            device_id_type=pl.DeviceIdType.MESH)

    def to_col(phase, i, src, dst):
        return pltpu.make_async_remote_copy(
            src_ref=src, dst_ref=dst, send_sem=ctx_send_sem.at[phase, i],
            recv_sem=ctx_recv_sem.at[phase, i], device_id={"ctx": cols[i]},
            device_id_type=pl.DeviceIdType.MESH)

    barrier = pltpu.get_barrier_semaphore()
    for i in range(1, data):
        pl.semaphore_signal(barrier, inc=1, device_id={"dp": ranks[i]}, device_id_type=pl.DeviceIdType.MESH)
    for i in range(1, ctx):
        pl.semaphore_signal(barrier, inc=1, device_id={"ctx": cols[i]}, device_id_type=pl.DeviceIdType.MESH)

    small = [
        pltpu.make_async_copy(src, dst, small_sem.at[n])
        for n, (src, dst) in enumerate((
            (route_hbm, route_ref), (doc_hbm, doc_ref), (k_hbm, k_ref), (q_hbm, q_ref), (g_hbm, g_ref)))]
    for copy in small:
        copy.start()
    loads = []
    for n in range(CHUNKS):
        span = pl.ds(n * step, step)
        loads.append((
            pltpu.make_async_copy(x_ref.at[:, span], x_buf.at[:, span], load_sem.at[0, n]),
            pltpu.make_async_copy(w_ref.at[span, :], w_buf.at[span, :], load_sem.at[1, n])))
        for load in loads[-1]:
            load.start()

    pl.semaphore_wait(barrier, data - 1 + ctx - 1)

    x_out, x_own = [], []
    for d in range(data if aligned else 1):
        for i in range(ctx):
            if aligned:
                start = pl.multiple_of((d * ctx + cols[i]) * block, block)
                source = x_ref.at[:, pl.ds(start, block)]
            else:
                source = cols_ref.at[cols[i]]
            if i == 0:
                x_own.append(pltpu.make_async_copy(source, x_recv.at[d, col], own_sem.at[d]))
            else:
                x_out.append(pltpu.make_async_remote_copy(
                    src_ref=source, dst_ref=x_recv.at[d, col],
                    send_sem=x_send_sem.at[d, i], recv_sem=x_recv_sem.at[d, i],
                    device_id={"ctx": cols[i]}, device_id_type=pl.DeviceIdType.MESH))
    for copy in x_own + x_out:
        copy.start()

    for copy in small[:3]:
        copy.wait()

    going = [[(route_ref[rank, 0, j] == ranks[i]).astype(F32) for j in range(groups)] for i in range(data)]
    if not direct:
        placed, before = [], 0
        for s in range(data):
            count = 0
            for j in range(groups):
                count = count + (route_ref[s, 0, j] == rank).astype(jnp.int32)
            placed.append([((before == k) & (count > 0)).astype(F32) for k in range(groups)])
            before = before + count

    def parts(array):
        return [array[j * size:(j + 1) * size] for j in range(groups)]

    k_parts = parts(k_ref[...])
    values = jnp.zeros((rows, head), F32)
    for n in range(CHUNKS):
        for load in loads[n]:
            load.wait()
        values = values + jnp.dot(
            x_buf[:, n * step:(n + 1) * step], w_buf[n * step:(n + 1) * step, :],
            preferred_element_type=F32)
    v_parts = parts(values.astype(BF16))
    for i in range(data):
        piece = jnp.concatenate([pick(going[i], k_parts), pick(going[i], v_parts)], axis=1)
        if i == 0:
            kv_recv[rank] = piece
        else:
            kv_send[i] = piece

    kv_out = [to_rank(KV, i, kv_send.at[i], kv_recv.at[rank]) for i in range(1, data)]
    for copy in kv_out:
        copy.start()
    small[3].wait()
    q_parts = parts(q_ref[...])
    q_out = []
    for i in range(1, data):
        q_send[i] = pick(going[i], q_parts)
        q_out.append(to_rank(Q, i, q_send.at[i], q_recv.at[rank]))
        q_out[-1].start()
    q_recv[rank] = pick(going[0], q_parts)
    def arrange(buffer):
        if direct:
            return buffer[...].reshape(rows, buffer.shape[2])
        pieces = [buffer[s] for s in range(data)]
        return jnp.concatenate(
            [pick([placed[s][k] for s in range(data)], pieces) for k in range(groups)], axis=0)

    for copy in kv_out:
        copy.wait_recv()
    kv_all[col] = arrange(kv_recv)
    gather = [to_col(GATHER, i, kv_all.at[col], kv_all.at[col]) for i in range(1, ctx)]
    for copy in gather:
        copy.start()
    small[4].wait()
    for copy in q_out:
        copy.wait_recv()
    queries = arrange(q_recv)
    for copy in gather:
        copy.wait_recv()

    scale = 1.0 / math.sqrt(head)
    pack_len = ctx * seg

    def stack(array, p):
        return jnp.concatenate(
            [array[p * seg:(p + 1) * seg, h * head:(h + 1) * head] for h in range(heads)], axis=0)

    scores_grad, query_stacks, key_stacks = [], [], []
    for p in range(packs):
        pair = kv_all[:, p * seg:(p + 1) * seg, :].reshape(pack_len, 2 * head)
        keys, vals = pair[:, :head], pair[:, head:]
        query_pos = col * seg + lax.broadcasted_iota(jnp.int32, (seg, pack_len), 0)
        key_pos = lax.broadcasted_iota(jnp.int32, (seg, pack_len), 1)
        query_doc, key_doc, end = jnp.zeros_like(query_pos), jnp.zeros_like(key_pos), 0
        for n in range(docs):
            end = end + doc_ref[p, n] * TILE
            query_doc = query_doc + jnp.where(query_pos >= end, 1, 0)
            key_doc = key_doc + jnp.where(key_pos >= end, 1, 0)
        bias = jnp.where((query_doc == key_doc) & (key_pos <= query_pos), 0.0, -1e30)
        query_stack, grad_stack = stack(queries, p), stack(g_ref, p)
        scores = contract_lanes(query_stack, keys) * scale
        scores = (scores.reshape(heads, seg, pack_len) + bias[None]).reshape(heads * seg, pack_len)
        weights = jnp.exp(scores - jnp.max(scores, axis=1, keepdims=True))
        probs = weights * (1.0 / jnp.sum(weights, axis=1, keepdims=True))
        grad_probs = contract_lanes(grad_stack, vals)
        inner = jnp.sum(probs * grad_probs, axis=1, keepdims=True)
        ds = (probs * (grad_probs - inner) * scale).astype(BF16)
        dk = contract_rows(ds, query_stack).astype(BF16)
        dv = contract_rows(probs.astype(BF16), grad_stack).astype(BF16)
        red_send[:, p * seg:(p + 1) * seg, :head] = dk.reshape(ctx, seg, head)
        red_send[:, p * seg:(p + 1) * seg, head:] = dv.reshape(ctx, seg, head)
        scores_grad.append(ds)
        key_stacks.append(keys)
    reduce = [to_col(REDUCE, i, red_send.at[cols[i]], red_recv.at[i]) for i in range(1, ctx)]
    for copy in reduce:
        copy.start()

    halves = []
    for p in range(packs):
        dq = jnp.dot(scores_grad[p], key_stacks[p], preferred_element_type=F32).astype(BF16)
        halves.append(jnp.concatenate([dq[h * seg:(h + 1) * seg] for h in range(heads)], axis=1))
    dq_rows = jnp.concatenate(halves, axis=0)

    def hand_back(array, send, recv, phase):
        if direct:
            send[...] = array.reshape(send.shape)
            recv[rank] = send[rank]
            copies = [to_rank(phase, i, send.at[ranks[i]], recv.at[rank]) for i in range(1, data)]
        else:
            pieces = parts(array)
            for s in range(data):
                send[s] = pick(placed[s], pieces)
            recv[rank] = send[rank]
            copies = [to_rank(phase, i, send.at[ranks[i]], recv.at[rank]) for i in range(1, data)]
        for copy in copies:
            copy.start()
        return copies

    def restore(recv):
        pieces = [recv[ranks[i]] for i in range(data)]
        return jnp.concatenate(
            [pick([going[i][j] for i in range(data)], pieces) for j in range(groups)], axis=0)

    dq_out = hand_back(dq_rows, dq_send, dq_recv, DQ)

    total = red_send[col].astype(F32)
    for copy in reduce:
        copy.wait_recv()
    for i in range(1, ctx):
        total = total + red_recv[i].astype(F32)
    dkv_out = hand_back(total.astype(BF16), dkv_send, dkv_recv, DKV)
    for copy in dkv_out:
        copy.wait_recv()
    dkv = restore(dkv_recv)
    vg_all[col] = dkv[:, head:]
    vgrad = [to_col(VGRAD, i, vg_all.at[col], vg_all.at[col]) for i in range(1, ctx)]
    for copy in vgrad:
        copy.start()
    kg_ref[...] = dkv[:, :head]
    for copy in x_out:
        copy.wait_recv()
    for copy in x_own:
        copy.wait()
    for copy in vgrad:
        copy.wait_recv()
    value_grad = vg_all[...].reshape(ctx * rows, head)
    wg_out = []
    if not aligned:
        terms = contract_rows(x_recv[0].reshape(ctx * rows, data * block), value_grad)
        wg_send[...] = terms.astype(BF16).reshape(wg_send.shape)
    for i in range(1, data):
        if aligned:
            term = contract_rows(value_grad, x_recv[ranks[i]].reshape(ctx * rows, block))
            wg_send[ranks[i]] = term.astype(BF16)
        copy = to_rank(WG, i, wg_send.at[ranks[i]], wg_recv.at[i])
        copy.start()
        wg_out.append(copy)
    if aligned:
        weight_grad = contract_rows(value_grad, x_recv[rank].reshape(ctx * rows, block))
    else:
        weight_grad = wg_send[rank].astype(F32)
    for copy in dq_out:
        copy.wait_recv()
    qg_ref[...] = restore(dq_recv)
    for copy in wg_out:
        copy.wait_recv()
    for i in range(1, data):
        weight_grad = weight_grad + wg_recv[i].astype(F32)
    wg_ref[...] = weight_grad.T if aligned else weight_grad
    for copy in kv_out + q_out + x_out + gather + reduce + dq_out + dkv_out + vgrad + wg_out:
        copy.wait_send()


def local(inputs, value_weight, queries, keys, out_grad, doc_tiles, route):
    data, ctx = lax.axis_size("dp"), lax.axis_size("ctx")
    rows, depth = inputs.shape
    head, width = keys.shape[1], queries.shape[1]
    groups = route.shape[2]
    size = rows // groups
    block = depth // (data * ctx)
    columns, blocks, term = inputs, (data, ctx, rows, block), (data, head, block)
    if block % 128:
        columns = jnp.transpose(inputs.reshape(rows, data, ctx, block), (2, 0, 1, 3))
        columns = columns.reshape(ctx, rows, data * block)
        blocks, term = (1, ctx, rows, data * block), (data, block, head)
    vmem = pl.BlockSpec(memory_space=pltpu.VMEM)
    hbm = pl.BlockSpec(memory_space=pltpu.HBM)
    dma = pltpu.SemaphoreType.DMA
    return pl.pallas_call(
        functools.partial(kernel, data, ctx),
        out_shape=(
            jax.ShapeDtypeStruct((rows, width), BF16),
            jax.ShapeDtypeStruct((rows, head), BF16),
            jax.ShapeDtypeStruct((block, head), F32)),
        in_specs=[hbm] * 8,
        out_specs=(vmem, vmem, vmem),
        scratch_shapes=[
            pltpu.VMEM((rows, depth), BF16),
            pltpu.VMEM((depth, head), BF16),
            pltpu.VMEM((rows, width), BF16),
            pltpu.VMEM((rows, head), BF16),
            pltpu.VMEM((rows, width), BF16),
            pltpu.SMEM(doc_tiles.shape, jnp.int32),
            pltpu.SMEM(route.shape, jnp.int32),
            pltpu.VMEM((data, size, 2 * head), BF16),
            pltpu.VMEM((data, size, 2 * head), BF16),
            pltpu.VMEM((data, size, width), BF16),
            pltpu.VMEM((data, size, width), BF16),
            pltpu.VMEM((ctx, rows, 2 * head), BF16),
            pltpu.VMEM(blocks, BF16),
            pltpu.VMEM((ctx, rows, 2 * head), BF16),
            pltpu.VMEM((ctx, rows, 2 * head), BF16),
            pltpu.VMEM((data, size, width), BF16),
            pltpu.VMEM((data, size, width), BF16),
            pltpu.VMEM((data, size, 2 * head), BF16),
            pltpu.VMEM((data, size, 2 * head), BF16),
            pltpu.VMEM((ctx, rows, head), BF16),
            pltpu.VMEM(term, BF16),
            pltpu.VMEM(term, BF16),
            dma((2, CHUNKS)), dma((5,)), dma((data,)),
            dma((5, data)), dma((5, data)), dma((3, ctx)), dma((3, ctx)),
            dma((data, ctx)), dma((data, ctx)),
        ],
        compiler_params=pltpu.CompilerParams(
            collective_id=0, has_side_effects=True, vmem_limit_bytes=65000 * 1024),
    )(inputs, columns, value_weight, queries, keys, out_grad, doc_tiles, route)


def solution(mesh):
    in_specs = (
        P(("dp", "ctx"), None),
        P(None, "tensor"),
        P(("dp", "ctx"), "tensor"),
        P(("dp", "ctx"), "tensor"),
        P(("dp", "ctx"), "tensor"),
        P("dp", None),
        P(None, "ctx", None),
    )
    out_specs = (P(("dp", "ctx"), "tensor"), P(("dp", "ctx"), "tensor"), P(("dp", "ctx"), "tensor"))
    return jax.shard_map(local, mesh=mesh, in_specs=in_specs, out_specs=out_specs, check_vma=False)
```

```python
import functools
import math

import jax
import jax.numpy as jnp
from jax import lax
from jax.experimental import pallas as pl
from jax.experimental.pallas import tpu as pltpu
from jax.sharding import PartitionSpec as P

TILE = 16
CHUNKS = 4
BF16 = jnp.bfloat16
F32 = jnp.float32
KV, Q, DQ, DKV, WG = range(5)
GATHER, REDUCE, VGRAD = range(3)


def contract_rows(left, right):
    return lax.dot_general(left, right, (((0,), (0,)), ((), ())), preferred_element_type=F32)


def contract_lanes(left, right):
    return lax.dot_general(left, right, (((1,), (1,)), ((), ())), preferred_element_type=F32)


def pick(flags, pieces):
    total = flags[0] * pieces[0].astype(F32)
    for flag, piece in zip(flags[1:], pieces[1:]):
        total = total + flag * piece.astype(F32)
    return total.astype(BF16)


def kernel(
    data, ctx, tensor, x_ref, cols_ref, w_ref, q_hbm, k_hbm, g_hbm, doc_hbm, route_hbm,
    qg_ref, kg_ref, wg_ref,
    x_buf, w_buf, q_ref, k_ref, g_ref, doc_ref, route_ref, kv_send, kv_recv, q_send, q_recv, kv_all, x_recv,
    red_send, red_recv, dq_send, dq_recv, dkv_send, dkv_recv, vg_all, wg_send, wg_recv,
    load_sem, small_sem, own_sem, dp_send_sem, dp_recv_sem, ctx_send_sem, ctx_recv_sem, x_send_sem, x_recv_sem,
):
    rank, col = lax.axis_index("dp"), lax.axis_index("ctx")
    rows, head = k_ref.shape
    width = q_ref.shape[1]
    heads = width // head
    groups = route_ref.shape[2]
    size = rows // groups
    packs, docs = doc_ref.shape
    seg = rows // packs
    block = wg_ref.shape[0]
    depth = x_ref.shape[1]
    step = depth // CHUNKS
    direct = groups == data
    aligned = block % 128 == 0
    ranks = [lax.rem(rank + i, data) for i in range(data)]
    shared = aligned and data % 2 == 0 and ctx % 2 == 0 and tensor % 2 == 0
    if ctx % 2 == 0:
        core, chip = lax.rem(col, 2), lax.div(col, 2)
        cores, chips = (core, 1 - core), ctx // 2
        cols = [2 * lax.rem(chip + i // 2, chips) + cores[i % 2] for i in range(ctx)]
        sources = [2 * lax.rem(chip + chips - i // 2, chips) + cores[i % 2] for i in range(ctx)]
    else:
        cols = [lax.rem(col + i, ctx) for i in range(ctx)]
    share = lax.axis_index("tensor")
    half = lax.rem(share, 2)
    partner = share + 1 - 2 * half

    def to_rank(phase, i, src, dst):
        return pltpu.make_async_remote_copy(
            src_ref=src, dst_ref=dst, send_sem=dp_send_sem.at[phase, i],
            recv_sem=dp_recv_sem.at[phase, i], device_id={"dp": ranks[i]},
            device_id_type=pl.DeviceIdType.MESH)

    def to_col(phase, i, src, dst):
        return pltpu.make_async_remote_copy(
            src_ref=src, dst_ref=dst, send_sem=ctx_send_sem.at[phase, i],
            recv_sem=ctx_recv_sem.at[phase, i], device_id={"ctx": cols[i]},
            device_id_type=pl.DeviceIdType.MESH)

    barrier = pltpu.get_barrier_semaphore()
    for i in range(1, data):
        pl.semaphore_signal(barrier, inc=1, device_id={"dp": ranks[i]}, device_id_type=pl.DeviceIdType.MESH)
    for i in range(1, ctx):
        pl.semaphore_signal(barrier, inc=1, device_id={"ctx": cols[i]}, device_id_type=pl.DeviceIdType.MESH)

    small = [
        pltpu.make_async_copy(src, dst, small_sem.at[n])
        for n, (src, dst) in enumerate((
            (route_hbm, route_ref), (doc_hbm, doc_ref), (k_hbm, k_ref), (q_hbm, q_ref), (g_hbm, g_ref)))]
    for copy in small:
        copy.start()
    if shared:
        pl.semaphore_signal(barrier, inc=1, device_id={"tensor": partner}, device_id_type=pl.DeviceIdType.MESH)
    loads = []
    for n in range(CHUNKS):
        span = pl.ds(n * step, step)
        loads.append((
            pltpu.make_async_copy(x_ref.at[:, span], x_buf.at[:, span], load_sem.at[0, n]),
            pltpu.make_async_copy(w_ref.at[span, :], w_buf.at[span, :], load_sem.at[1, n])))
        for load in loads[-1]:
            load.start()

    pl.semaphore_wait(barrier, data - 1 + ctx - 1 + (1 if shared else 0))

    x_out, x_own, x_direct, x_forward = [], [], [], []

    def columns(d, i):
        if not aligned:
            return cols_ref.at[cols[i]]
        return x_ref.at[:, pl.ds(pl.multiple_of((d * ctx + cols[i]) * block, block), block)]

    def exchange(src, dst, k, i, device):
        return pltpu.make_async_remote_copy(
            src_ref=src, dst_ref=dst, send_sem=x_send_sem.at[k, i], recv_sem=x_recv_sem.at[k, i],
            device_id=device, device_id_type=pl.DeviceIdType.MESH)

    for d in range(data if aligned else 1):
        x_own.append(pltpu.make_async_copy(columns(d, 0), x_recv.at[d, col], own_sem.at[d]))
        for i in range(1, 2 if shared else ctx):
            x_out.append(exchange(columns(d, i), x_recv.at[d, col], d, i, {"ctx": cols[i]}))
    if shared:
        for k in range(data // 2):
            d = 2 * k + half
            for i in range(2, ctx):
                x_direct.append(exchange(columns(d, i), x_recv.at[d, col], k, i, {"ctx": cols[i]}))
                place = x_recv.at[d, sources[i]]
                x_forward.append(exchange(place, place, data // 2 + k, i, {"tensor": partner}))
    middle = len(x_direct) // 2

    def hand_on(first, last):
        for n in range(first, last):
            x_direct[n].wait_recv()
            x_forward[n].start()

    for copy in x_direct + x_own + x_out:
        copy.start()

    for copy in small[:3]:
        copy.wait()

    going = [[(route_ref[rank, 0, j] == ranks[i]).astype(F32) for j in range(groups)] for i in range(data)]
    if not direct:
        placed, before = [], 0
        for s in range(data):
            count = 0
            for j in range(groups):
                count = count + (route_ref[s, 0, j] == rank).astype(jnp.int32)
            placed.append([((before == k) & (count > 0)).astype(F32) for k in range(groups)])
            before = before + count

    def parts(array):
        return [array[j * size:(j + 1) * size] for j in range(groups)]

    k_parts = parts(k_ref[...])
    values = jnp.zeros((rows, head), F32)
    for n in range(CHUNKS):
        for load in loads[n]:
            load.wait()
        values = values + jnp.dot(
            x_buf[:, n * step:(n + 1) * step], w_buf[n * step:(n + 1) * step, :],
            preferred_element_type=F32)
    v_parts = parts(values.astype(BF16))
    for i in range(data):
        piece = jnp.concatenate([pick(going[i], k_parts), pick(going[i], v_parts)], axis=1)
        if i == 0:
            kv_recv[rank] = piece
        else:
            kv_send[i] = piece

    kv_out = [to_rank(KV, i, kv_send.at[i], kv_recv.at[rank]) for i in range(1, data)]
    for copy in kv_out:
        copy.start()
    small[3].wait()
    q_parts = parts(q_ref[...])
    q_out = []
    for i in range(1, data):
        q_send[i] = pick(going[i], q_parts)
        q_out.append(to_rank(Q, i, q_send.at[i], q_recv.at[rank]))
        q_out[-1].start()
    q_recv[rank] = pick(going[0], q_parts)
    def arrange(buffer):
        if direct:
            return buffer[...].reshape(rows, buffer.shape[2])
        pieces = [buffer[s] for s in range(data)]
        return jnp.concatenate(
            [pick([placed[s][k] for s in range(data)], pieces) for k in range(groups)], axis=0)

    for copy in kv_out:
        copy.wait_recv()
    kv_all[col] = arrange(kv_recv)
    gather = [to_col(GATHER, i, kv_all.at[col], kv_all.at[col]) for i in range(1, ctx)]
    for copy in gather:
        copy.start()
    small[4].wait()
    for copy in q_out:
        copy.wait_recv()
    queries = arrange(q_recv)
    for copy in gather:
        copy.wait_recv()
    hand_on(0, middle)

    scale = 1.0 / math.sqrt(head)
    pack_len = ctx * seg

    def stack(array, p):
        return jnp.concatenate(
            [array[p * seg:(p + 1) * seg, h * head:(h + 1) * head] for h in range(heads)], axis=0)

    scores_grad, query_stacks, key_stacks = [], [], []
    for p in range(packs):
        pair = kv_all[:, p * seg:(p + 1) * seg, :].reshape(pack_len, 2 * head)
        keys, vals = pair[:, :head], pair[:, head:]
        query_pos = col * seg + lax.broadcasted_iota(jnp.int32, (seg, pack_len), 0)
        key_pos = lax.broadcasted_iota(jnp.int32, (seg, pack_len), 1)
        query_doc, key_doc, end = jnp.zeros_like(query_pos), jnp.zeros_like(key_pos), 0
        for n in range(docs):
            end = end + doc_ref[p, n] * TILE
            query_doc = query_doc + jnp.where(query_pos >= end, 1, 0)
            key_doc = key_doc + jnp.where(key_pos >= end, 1, 0)
        bias = jnp.where((query_doc == key_doc) & (key_pos <= query_pos), 0.0, -1e30)
        query_stack, grad_stack = stack(queries, p), stack(g_ref, p)
        scores = contract_lanes(query_stack, keys) * scale
        scores = (scores.reshape(heads, seg, pack_len) + bias[None]).reshape(heads * seg, pack_len)
        weights = jnp.exp(scores - jnp.max(scores, axis=1, keepdims=True))
        probs = weights * (1.0 / jnp.sum(weights, axis=1, keepdims=True))
        grad_probs = contract_lanes(grad_stack, vals)
        inner = jnp.sum(probs * grad_probs, axis=1, keepdims=True)
        ds = (probs * (grad_probs - inner) * scale).astype(BF16)
        dk = contract_rows(ds, query_stack).astype(BF16)
        dv = contract_rows(probs.astype(BF16), grad_stack).astype(BF16)
        red_send[:, p * seg:(p + 1) * seg, :head] = dk.reshape(ctx, seg, head)
        red_send[:, p * seg:(p + 1) * seg, head:] = dv.reshape(ctx, seg, head)
        scores_grad.append(ds)
        key_stacks.append(keys)
    reduce = [to_col(REDUCE, i, red_send.at[cols[i]], red_recv.at[i]) for i in range(1, ctx)]
    for copy in reduce:
        copy.start()
    hand_on(middle, len(x_direct))

    halves = []
    for p in range(packs):
        dq = jnp.dot(scores_grad[p], key_stacks[p], preferred_element_type=F32).astype(BF16)
        halves.append(jnp.concatenate([dq[h * seg:(h + 1) * seg] for h in range(heads)], axis=1))
    dq_rows = jnp.concatenate(halves, axis=0)

    def hand_back(array, send, recv, phase):
        if direct:
            send[...] = array.reshape(send.shape)
            recv[rank] = send[rank]
            copies = [to_rank(phase, i, send.at[ranks[i]], recv.at[rank]) for i in range(1, data)]
        else:
            pieces = parts(array)
            for s in range(data):
                send[s] = pick(placed[s], pieces)
            recv[rank] = send[rank]
            copies = [to_rank(phase, i, send.at[ranks[i]], recv.at[rank]) for i in range(1, data)]
        for copy in copies:
            copy.start()
        return copies

    def restore(recv):
        pieces = [recv[ranks[i]] for i in range(data)]
        return jnp.concatenate(
            [pick([going[i][j] for i in range(data)], pieces) for j in range(groups)], axis=0)

    dq_out = hand_back(dq_rows, dq_send, dq_recv, DQ)

    total = red_send[col].astype(F32)
    for copy in reduce:
        copy.wait_recv()
    for i in range(1, ctx):
        total = total + red_recv[i].astype(F32)
    dkv_out = hand_back(total.astype(BF16), dkv_send, dkv_recv, DKV)
    for copy in dkv_out:
        copy.wait_recv()
    dkv = restore(dkv_recv)
    vg_all[col] = dkv[:, head:]
    vgrad = [to_col(VGRAD, i, vg_all.at[col], vg_all.at[col]) for i in range(1, ctx)]
    for copy in vgrad:
        copy.start()
    kg_ref[...] = dkv[:, :head]
    for copy in x_out + x_forward:
        copy.wait_recv()
    for copy in x_own:
        copy.wait()
    for copy in vgrad:
        copy.wait_recv()
    value_grad = vg_all[...].reshape(ctx * rows, head)
    wg_out = []
    if not aligned:
        terms = contract_rows(x_recv[0].reshape(ctx * rows, data * block), value_grad)
        wg_send[...] = terms.astype(BF16).reshape(wg_send.shape)
    for i in range(1, data):
        if aligned:
            term = contract_rows(value_grad, x_recv[ranks[i]].reshape(ctx * rows, block))
            wg_send[ranks[i]] = term.astype(BF16)
        copy = to_rank(WG, i, wg_send.at[ranks[i]], wg_recv.at[i])
        copy.start()
        wg_out.append(copy)
    if aligned:
        weight_grad = contract_rows(value_grad, x_recv[rank].reshape(ctx * rows, block))
    else:
        weight_grad = wg_send[rank].astype(F32)
    for copy in dq_out:
        copy.wait_recv()
    qg_ref[...] = restore(dq_recv)
    for copy in wg_out:
        copy.wait_recv()
    for i in range(1, data):
        weight_grad = weight_grad + wg_recv[i].astype(F32)
    wg_ref[...] = weight_grad.T if aligned else weight_grad
    for copy in kv_out + q_out + x_out + x_direct + x_forward + gather + reduce + dq_out + dkv_out + vgrad + wg_out:
        copy.wait_send()


def local(inputs, value_weight, queries, keys, out_grad, doc_tiles, route):
    data, ctx = lax.axis_size("dp"), lax.axis_size("ctx")
    rows, depth = inputs.shape
    head, width = keys.shape[1], queries.shape[1]
    groups = route.shape[2]
    size = rows // groups
    block = depth // (data * ctx)
    columns, blocks, term = inputs, (data, ctx, rows, block), (data, head, block)
    if block % 128:
        columns = jnp.transpose(inputs.reshape(rows, data, ctx, block), (2, 0, 1, 3))
        columns = columns.reshape(ctx, rows, data * block)
        blocks, term = (1, ctx, rows, data * block), (data, block, head)
    vmem = pl.BlockSpec(memory_space=pltpu.VMEM)
    hbm = pl.BlockSpec(memory_space=pltpu.HBM)
    dma = pltpu.SemaphoreType.DMA
    return pl.pallas_call(
        functools.partial(kernel, data, ctx, lax.axis_size("tensor")),
        out_shape=(
            jax.ShapeDtypeStruct((rows, width), BF16),
            jax.ShapeDtypeStruct((rows, head), BF16),
            jax.ShapeDtypeStruct((block, head), F32)),
        in_specs=[hbm] * 8,
        out_specs=(vmem, vmem, vmem),
        scratch_shapes=[
            pltpu.VMEM((rows, depth), BF16),
            pltpu.VMEM((depth, head), BF16),
            pltpu.VMEM((rows, width), BF16),
            pltpu.VMEM((rows, head), BF16),
            pltpu.VMEM((rows, width), BF16),
            pltpu.SMEM(doc_tiles.shape, jnp.int32),
            pltpu.SMEM(route.shape, jnp.int32),
            pltpu.VMEM((data, size, 2 * head), BF16),
            pltpu.VMEM((data, size, 2 * head), BF16),
            pltpu.VMEM((data, size, width), BF16),
            pltpu.VMEM((data, size, width), BF16),
            pltpu.VMEM((ctx, rows, 2 * head), BF16),
            pltpu.VMEM(blocks, BF16),
            pltpu.VMEM((ctx, rows, 2 * head), BF16),
            pltpu.VMEM((ctx, rows, 2 * head), BF16),
            pltpu.VMEM((data, size, width), BF16),
            pltpu.VMEM((data, size, width), BF16),
            pltpu.VMEM((data, size, 2 * head), BF16),
            pltpu.VMEM((data, size, 2 * head), BF16),
            pltpu.VMEM((ctx, rows, head), BF16),
            pltpu.VMEM(term, BF16),
            pltpu.VMEM(term, BF16),
            dma((2, CHUNKS)), dma((5,)), dma((data,)),
            dma((5, data)), dma((5, data)), dma((3, ctx)), dma((3, ctx)),
            dma((data, ctx)), dma((data, ctx)),
        ],
        compiler_params=pltpu.CompilerParams(
            collective_id=0, has_side_effects=True, vmem_limit_bytes=65000 * 1024),
    )(inputs, columns, value_weight, queries, keys, out_grad, doc_tiles, route)


def solution(mesh):
    in_specs = (
        P(("dp", "ctx"), None),
        P(None, "tensor"),
        P(("dp", "ctx"), "tensor"),
        P(("dp", "ctx"), "tensor"),
        P(("dp", "ctx"), "tensor"),
        P("dp", None),
        P(None, "ctx", None),
    )
    out_specs = (P(("dp", "ctx"), "tensor"), P(("dp", "ctx"), "tensor"), P(("dp", "ctx"), "tensor"))
    return jax.shard_map(local, mesh=mesh, in_specs=in_specs, out_specs=out_specs, check_vma=False)
```

```python
import functools
import math

import jax
import jax.numpy as jnp
from jax import lax
from jax.experimental import pallas as pl
from jax.experimental.pallas import tpu as pltpu
from jax.sharding import PartitionSpec as P

TILE = 16
CHUNKS = 4
BF16 = jnp.bfloat16
F32 = jnp.float32
KV, Q, DQ, DKV, WG = range(5)
GATHER, REDUCE, VGRAD = range(3)


def contract_rows(left, right):
    return lax.dot_general(left, right, (((0,), (0,)), ((), ())), preferred_element_type=F32)


def contract_lanes(left, right):
    return lax.dot_general(left, right, (((1,), (1,)), ((), ())), preferred_element_type=F32)


def pick(flags, pieces):
    total = flags[0] * pieces[0].astype(F32)
    for flag, piece in zip(flags[1:], pieces[1:]):
        total = total + flag * piece.astype(F32)
    return total.astype(BF16)


def kernel(
    data, ctx, tensor, x_ref, cols_ref, w_ref, q_hbm, k_hbm, g_hbm, doc_hbm, route_hbm,
    qg_ref, kg_ref, wg_ref,
    x_buf, w_buf, q_ref, k_ref, g_ref, doc_ref, route_ref, kv_send, kv_recv, q_send, q_recv, kv_all, x_recv,
    red_send, red_recv, dq_send, dq_recv, dkv_send, dkv_recv, vg_all, wg_send, wg_recv,
    load_sem, small_sem, own_sem, dp_send_sem, dp_recv_sem, ctx_send_sem, ctx_recv_sem, x_send_sem, x_recv_sem,
):
    rank, col = lax.axis_index("dp"), lax.axis_index("ctx")
    rows, head = k_ref.shape
    width = q_ref.shape[1]
    heads = width // head
    groups = route_ref.shape[2]
    size = rows // groups
    packs, docs = doc_ref.shape
    seg = rows // packs
    block = wg_ref.shape[0]
    depth = x_ref.shape[1]
    step = depth // CHUNKS
    direct = groups == data
    aligned = block % 128 == 0
    ranks = [lax.rem(rank + i, data) for i in range(data)]
    shared = aligned and data % 2 == 0 and ctx % 2 == 0 and tensor % 2 == 0
    if ctx % 2 == 0:
        core, chip = lax.rem(col, 2), lax.div(col, 2)
        cores, chips = (core, 1 - core), ctx // 2
        cols = [2 * lax.rem(chip + i // 2, chips) + cores[i % 2] for i in range(ctx)]
        sources = [2 * lax.rem(chip + chips - i // 2, chips) + cores[i % 2] for i in range(ctx)]
    else:
        cols = [lax.rem(col + i, ctx) for i in range(ctx)]
    share = lax.axis_index("tensor")
    half = lax.rem(share, 2)
    partner = share + 1 - 2 * half

    def to_rank(phase, i, src, dst):
        return pltpu.make_async_remote_copy(
            src_ref=src, dst_ref=dst, send_sem=dp_send_sem.at[phase, i],
            recv_sem=dp_recv_sem.at[phase, i], device_id={"dp": ranks[i]},
            device_id_type=pl.DeviceIdType.MESH)

    def to_col(phase, i, src, dst):
        return pltpu.make_async_remote_copy(
            src_ref=src, dst_ref=dst, send_sem=ctx_send_sem.at[phase, i],
            recv_sem=ctx_recv_sem.at[phase, i], device_id={"ctx": cols[i]},
            device_id_type=pl.DeviceIdType.MESH)

    barrier = pltpu.get_barrier_semaphore()
    for i in range(1, data):
        pl.semaphore_signal(barrier, inc=1, device_id={"dp": ranks[i]}, device_id_type=pl.DeviceIdType.MESH)
    for i in range(1, ctx):
        pl.semaphore_signal(barrier, inc=1, device_id={"ctx": cols[i]}, device_id_type=pl.DeviceIdType.MESH)

    small = [
        pltpu.make_async_copy(src, dst, small_sem.at[n])
        for n, (src, dst) in enumerate((
            (route_hbm, route_ref), (doc_hbm, doc_ref), (k_hbm, k_ref), (q_hbm, q_ref), (g_hbm, g_ref)))]
    for copy in small:
        copy.start()
    if shared:
        pl.semaphore_signal(barrier, inc=1, device_id={"tensor": partner}, device_id_type=pl.DeviceIdType.MESH)
    loads = []
    for n in range(CHUNKS):
        span = pl.ds(n * step, step)
        loads.append((
            pltpu.make_async_copy(x_ref.at[:, span], x_buf.at[:, span], load_sem.at[0, n]),
            pltpu.make_async_copy(w_ref.at[span, :], w_buf.at[span, :], load_sem.at[1, n])))
        for load in loads[-1]:
            load.start()

    pl.semaphore_wait(barrier, data - 1 + ctx - 1 + (1 if shared else 0))

    x_out, x_own, x_direct, x_forward = [], [], [], []

    def columns(d, i):
        if not aligned:
            return cols_ref.at[cols[i]]
        return x_ref.at[:, pl.ds(pl.multiple_of((d * ctx + cols[i]) * block, block), block)]

    def exchange(src, dst, k, i, device):
        return pltpu.make_async_remote_copy(
            src_ref=src, dst_ref=dst, send_sem=x_send_sem.at[k, i], recv_sem=x_recv_sem.at[k, i],
            device_id=device, device_id_type=pl.DeviceIdType.MESH)

    for d in range(data if aligned else 1):
        x_own.append(pltpu.make_async_copy(columns(d, 0), x_recv.at[d, col], own_sem.at[d]))
        for i in range(1, 2 if shared else ctx):
            x_out.append(exchange(columns(d, i), x_recv.at[d, col], d, i, {"ctx": cols[i]}))
    if shared:
        for k in range(data // 2):
            d = 2 * k + half
            for i in range(2, ctx):
                x_direct.append(exchange(columns(d, i), x_recv.at[d, col], k, i, {"ctx": cols[i]}))
                place = x_recv.at[d, sources[i]]
                x_forward.append(exchange(place, place, data // 2 + k, i, {"tensor": partner}))
    middle = len(x_direct) // 2

    def hand_on(first, last):
        for n in range(first, last):
            x_direct[n].wait_recv()
            x_forward[n].start()

    for copy in x_direct + x_own + x_out:
        copy.start()

    for copy in small[:3]:
        copy.wait()

    going = [[(route_ref[rank, 0, j] == ranks[i]).astype(F32) for j in range(groups)] for i in range(data)]
    if not direct:
        placed, before = [], 0
        for s in range(data):
            count = 0
            for j in range(groups):
                count = count + (route_ref[s, 0, j] == rank).astype(jnp.int32)
            placed.append([((before == k) & (count > 0)).astype(F32) for k in range(groups)])
            before = before + count

    def parts(array):
        return [array[j * size:(j + 1) * size] for j in range(groups)]

    k_parts = parts(k_ref[...])
    values = jnp.zeros((rows, head), F32)
    for n in range(CHUNKS):
        for load in loads[n]:
            load.wait()
        values = values + jnp.dot(
            x_buf[:, n * step:(n + 1) * step], w_buf[n * step:(n + 1) * step, :],
            preferred_element_type=F32)
    v_parts = parts(values.astype(BF16))
    for i in range(data):
        piece = jnp.concatenate([pick(going[i], k_parts), pick(going[i], v_parts)], axis=1)
        if i == 0:
            kv_recv[rank] = piece
        else:
            kv_send[i] = piece

    kv_out = [to_rank(KV, i, kv_send.at[i], kv_recv.at[rank]) for i in range(1, data)]
    for copy in kv_out:
        copy.start()
    small[3].wait()
    q_parts = parts(q_ref[...])
    q_out = []
    for i in range(1, data):
        q_send[i] = pick(going[i], q_parts)
        q_out.append(to_rank(Q, i, q_send.at[i], q_recv.at[rank]))
        q_out[-1].start()
    q_recv[rank] = pick(going[0], q_parts)
    def arrange(buffer):
        if direct:
            return buffer[...].reshape(rows, buffer.shape[2])
        pieces = [buffer[s] for s in range(data)]
        return jnp.concatenate(
            [pick([placed[s][k] for s in range(data)], pieces) for k in range(groups)], axis=0)

    for copy in kv_out:
        copy.wait_recv()
    kv_all[col] = arrange(kv_recv)
    gather = [to_col(GATHER, i, kv_all.at[col], kv_all.at[col]) for i in range(1, ctx)]
    for copy in gather:
        copy.start()
    small[4].wait()
    for copy in q_out:
        copy.wait_recv()
    queries = arrange(q_recv)
    for copy in gather:
        copy.wait_recv()
    hand_on(0, middle)

    scale = 1.0 / math.sqrt(head)
    pack_len = ctx * seg

    def stack(array, p):
        return jnp.concatenate(
            [array[p * seg:(p + 1) * seg, h * head:(h + 1) * head] for h in range(heads)], axis=0)

    scores_grad, query_stacks, key_stacks = [], [], []
    for p in range(packs):
        pair = kv_all[:, p * seg:(p + 1) * seg, :].reshape(pack_len, 2 * head)
        keys, vals = pair[:, :head], pair[:, head:]
        query_pos = col * seg + lax.broadcasted_iota(jnp.int32, (seg, pack_len), 0)
        key_pos = lax.broadcasted_iota(jnp.int32, (seg, pack_len), 1)
        query_doc, key_doc, end = jnp.zeros_like(query_pos), jnp.zeros_like(key_pos), 0
        for n in range(docs):
            end = end + doc_ref[p, n] * TILE
            query_doc = query_doc + jnp.where(query_pos >= end, 1, 0)
            key_doc = key_doc + jnp.where(key_pos >= end, 1, 0)
        bias = jnp.where((query_doc == key_doc) & (key_pos <= query_pos), 0.0, -1e30)
        query_stack, grad_stack = stack(queries, p), stack(g_ref, p)
        scores = contract_lanes(query_stack, keys) * scale
        scores = (scores.reshape(heads, seg, pack_len) + bias[None]).reshape(heads * seg, pack_len)
        weights = jnp.exp(scores - jnp.max(scores, axis=1, keepdims=True))
        probs = weights * (1.0 / jnp.sum(weights, axis=1, keepdims=True))
        grad_probs = contract_lanes(grad_stack, vals)
        inner = jnp.sum(probs * grad_probs, axis=1, keepdims=True)
        ds = (probs * (grad_probs - inner) * scale).astype(BF16)
        dk = contract_rows(ds, query_stack).astype(BF16)
        dv = contract_rows(probs.astype(BF16), grad_stack).astype(BF16)
        red_send[:, p * seg:(p + 1) * seg, :head] = dk.reshape(ctx, seg, head)
        red_send[:, p * seg:(p + 1) * seg, head:] = dv.reshape(ctx, seg, head)
        scores_grad.append(ds)
        key_stacks.append(keys)
        if p == 0:
            hand_on(middle, len(x_direct))
    reduce = [to_col(REDUCE, i, red_send.at[cols[i]], red_recv.at[i]) for i in range(1, ctx)]
    for copy in reduce:
        copy.start()

    halves = []
    for p in range(packs):
        dq = jnp.dot(scores_grad[p], key_stacks[p], preferred_element_type=F32).astype(BF16)
        halves.append(jnp.concatenate([dq[h * seg:(h + 1) * seg] for h in range(heads)], axis=1))
    dq_rows = jnp.concatenate(halves, axis=0)

    def hand_back(array, send, recv, phase):
        if direct:
            send[...] = array.reshape(send.shape)
            recv[rank] = send[rank]
            copies = [to_rank(phase, i, send.at[ranks[i]], recv.at[rank]) for i in range(1, data)]
        else:
            pieces = parts(array)
            for s in range(data):
                send[s] = pick(placed[s], pieces)
            recv[rank] = send[rank]
            copies = [to_rank(phase, i, send.at[ranks[i]], recv.at[rank]) for i in range(1, data)]
        for copy in copies:
            copy.start()
        return copies

    def restore(recv):
        pieces = [recv[ranks[i]] for i in range(data)]
        return jnp.concatenate(
            [pick([going[i][j] for i in range(data)], pieces) for j in range(groups)], axis=0)

    dq_out = hand_back(dq_rows, dq_send, dq_recv, DQ)

    total = red_send[col].astype(F32)
    for copy in reduce:
        copy.wait_recv()
    for i in range(1, ctx):
        total = total + red_recv[i].astype(F32)
    dkv_out = hand_back(total.astype(BF16), dkv_send, dkv_recv, DKV)
    for copy in dkv_out:
        copy.wait_recv()
    dkv = restore(dkv_recv)
    vg_all[col] = dkv[:, head:]
    vgrad = [to_col(VGRAD, i, vg_all.at[col], vg_all.at[col]) for i in range(1, ctx)]
    for copy in vgrad:
        copy.start()
    kg_ref[...] = dkv[:, :head]
    for copy in x_out + x_forward:
        copy.wait_recv()
    for copy in x_own:
        copy.wait()
    for copy in vgrad:
        copy.wait_recv()
    value_grad = vg_all[...].reshape(ctx * rows, head)
    wg_out = []
    if not aligned:
        terms = contract_rows(x_recv[0].reshape(ctx * rows, data * block), value_grad)
        wg_send[...] = terms.astype(BF16).reshape(wg_send.shape)
    for i in range(1, data):
        if aligned:
            term = contract_rows(value_grad, x_recv[ranks[i]].reshape(ctx * rows, block))
            wg_send[ranks[i]] = term.astype(BF16)
        copy = to_rank(WG, i, wg_send.at[ranks[i]], wg_recv.at[i])
        copy.start()
        wg_out.append(copy)
    if aligned:
        weight_grad = contract_rows(value_grad, x_recv[rank].reshape(ctx * rows, block))
    else:
        weight_grad = wg_send[rank].astype(F32)
    for copy in dq_out:
        copy.wait_recv()
    qg_ref[...] = restore(dq_recv)
    for copy in wg_out:
        copy.wait_recv()
    for i in range(1, data):
        weight_grad = weight_grad + wg_recv[i].astype(F32)
    wg_ref[...] = weight_grad.T if aligned else weight_grad
    for copy in kv_out + q_out + x_out + x_direct + x_forward + gather + reduce + dq_out + dkv_out + vgrad + wg_out:
        copy.wait_send()


def local(inputs, value_weight, queries, keys, out_grad, doc_tiles, route):
    data, ctx = lax.axis_size("dp"), lax.axis_size("ctx")
    rows, depth = inputs.shape
    head, width = keys.shape[1], queries.shape[1]
    groups = route.shape[2]
    size = rows // groups
    block = depth // (data * ctx)
    columns, blocks, term = inputs, (data, ctx, rows, block), (data, head, block)
    if block % 128:
        columns = jnp.transpose(inputs.reshape(rows, data, ctx, block), (2, 0, 1, 3))
        columns = columns.reshape(ctx, rows, data * block)
        blocks, term = (1, ctx, rows, data * block), (data, block, head)
    vmem = pl.BlockSpec(memory_space=pltpu.VMEM)
    hbm = pl.BlockSpec(memory_space=pltpu.HBM)
    dma = pltpu.SemaphoreType.DMA
    return pl.pallas_call(
        functools.partial(kernel, data, ctx, lax.axis_size("tensor")),
        out_shape=(
            jax.ShapeDtypeStruct((rows, width), BF16),
            jax.ShapeDtypeStruct((rows, head), BF16),
            jax.ShapeDtypeStruct((block, head), F32)),
        in_specs=[hbm] * 8,
        out_specs=(vmem, vmem, vmem),
        scratch_shapes=[
            pltpu.VMEM((rows, depth), BF16),
            pltpu.VMEM((depth, head), BF16),
            pltpu.VMEM((rows, width), BF16),
            pltpu.VMEM((rows, head), BF16),
            pltpu.VMEM((rows, width), BF16),
            pltpu.SMEM(doc_tiles.shape, jnp.int32),
            pltpu.SMEM(route.shape, jnp.int32),
            pltpu.VMEM((data, size, 2 * head), BF16),
            pltpu.VMEM((data, size, 2 * head), BF16),
            pltpu.VMEM((data, size, width), BF16),
            pltpu.VMEM((data, size, width), BF16),
            pltpu.VMEM((ctx, rows, 2 * head), BF16),
            pltpu.VMEM(blocks, BF16),
            pltpu.VMEM((ctx, rows, 2 * head), BF16),
            pltpu.VMEM((ctx, rows, 2 * head), BF16),
            pltpu.VMEM((data, size, width), BF16),
            pltpu.VMEM((data, size, width), BF16),
            pltpu.VMEM((data, size, 2 * head), BF16),
            pltpu.VMEM((data, size, 2 * head), BF16),
            pltpu.VMEM((ctx, rows, head), BF16),
            pltpu.VMEM(term, BF16),
            pltpu.VMEM(term, BF16),
            dma((2, CHUNKS)), dma((5,)), dma((data,)),
            dma((5, data)), dma((5, data)), dma((3, ctx)), dma((3, ctx)),
            dma((data, ctx)), dma((data, ctx)),
        ],
        compiler_params=pltpu.CompilerParams(
            collective_id=0, has_side_effects=True, vmem_limit_bytes=65000 * 1024),
    )(inputs, columns, value_weight, queries, keys, out_grad, doc_tiles, route)


def solution(mesh):
    in_specs = (
        P(("dp", "ctx"), None),
        P(None, "tensor"),
        P(("dp", "ctx"), "tensor"),
        P(("dp", "ctx"), "tensor"),
        P(("dp", "ctx"), "tensor"),
        P("dp", None),
        P(None, "ctx", None),
    )
    out_specs = (P(("dp", "ctx"), "tensor"), P(("dp", "ctx"), "tensor"), P(("dp", "ctx"), "tensor"))
    return jax.shard_map(local, mesh=mesh, in_specs=in_specs, out_specs=out_specs, check_vma=False)
```
